256 devices in a mesh: blk: 8 (over y, x_lo), dp: 32 (over x_hi, z, core).
Axes of the slice: x: 4 (x_hi: 2, x_lo: 2; x = x_hi * 2 + x_lo), y: 4, z: 8, core: 2. Of those that a mesh axis runs over, the one named last changes fastest.
Arguments:
- image_feats: bfloat16 [131072, 1152], P(('blk', 'dp')), may hold values from -24 to 24
- text_feats: bfloat16 [131072, 1152], P(('blk', 'dp')), may hold values from -24 to 24
- image_head: bfloat16 [1152, 1152], replicated, may hold values from -0.1875 to 0.1875
- text_head: bfloat16 [1152, 1152], replicated, may hold values from -0.1875 to 0.1875
Outputs:
- row_loss: float32 [131072], P(('blk', 'dp'))
- image_head_grad: float32 [1152, 1152], P('dp', 'blk')
- text_head_grad: float32 [1152, 1152], P('dp', 'blk')
The draws below stay inside these ranges and needn't reach their ends.
All inputs are finite; a program needn't handle non-finite values.
Results may differ from the reference program's by a relative error of at most 0.0026.
Values may be sent and summed in bfloat16 or wider, within the bound.
No kernel may reach another device: no remote copies, remote signals or barrier semaphores. Data moves between devices by JAX's collectives and lax.ppermute only.
A program may use at most 128 MiB of HBM per device.

```python
import jax
import jax.numpy as jnp
from jax import lax

D = 1152
ROWS = 512
BATCH = 131072
N_BLK = 8
N_DP = 32


def with_spikes(drawn, own_key, source, target, blocks, factor):
    owner, partner = [(jnp.arange(drawn.shape[axis_at]) // (drawn.shape[axis_at] // blocks)).reshape([-1 if axis == axis_at else 1 for axis in range(drawn.ndim)]) for axis_at in (source, target)]
    chosen = jax.random.permutation(own_key, blocks)[partner]
    strong = (owner == chosen) | (owner == (partner + blocks // 2) % blocks)
    return jnp.where(strong, factor * drawn, drawn)


def level_of(own_key, dims, pieces, smallest, high):
    loudness, own = 1.0, jax.random.fold_in(own_key, 6)
    for position, blocks in pieces:
        steps = jnp.exp(jax.random.uniform(jax.random.fold_in(own, position), (blocks,), jnp.float32, smallest / len(pieces), high / len(pieces)))
        loudness = loudness * jnp.repeat(steps, dims[position] // blocks).reshape([-1 if axis == position else 1 for axis in range(len(dims))])
    return loudness


def normal_values(key, extent, scale, reach, split=(), kind=jnp.bfloat16):
    loudness = level_of(key, extent, split, -0.22, 0.18) if split else 1.0
    array = jax.random.normal(key, extent, jnp.float32) * scale * loudness
    return jnp.minimum(jnp.maximum(array, -reach), reach).astype(kind)


def heavy_noise(own_key, dims, width, most, pieces, heavy, kind=jnp.bfloat16):
    values = width * jax.random.normal(own_key, dims, jnp.float32)
    if pieces:
        values = values * level_of(own_key, dims, pieces, -0.22, 0.18)
    return jnp.clip(with_spikes(values, jax.random.fold_in(own_key, 3), *heavy), -most, most).astype(kind)


def setup_inputs(seed: int = 0) -> dict:
    keys = jax.random.split(jax.random.key(seed), 5)
    return {
        "image_feats": heavy_noise(keys[0], (BATCH, D), 1.0, 24.0, ((0, 256),), (0, 1, 128, 5.5)),
        "text_feats": heavy_noise(keys[1], (BATCH, D), 1.0, 24.0, ((0, 256),), (0, 1, 128, 5.5)),
        "image_head": normal_values(keys[2], (D, D), D ** -0.5, 0.1875),
        "text_head": normal_values(keys[3], (D, D), D ** -0.5, 0.1875),
    }


TEMP = 30.0
BIAS = -6.0
EPS = 1e-06

def embed(feats, head):
    proj = jnp.dot(feats, head, preferred_element_type=jnp.float32)
    norm = jnp.sqrt(lax.optimization_barrier(jnp.sum(proj * proj, axis=1, keepdims=True)) + EPS)
    return (proj / norm, norm)

def pair_terms(image_emb, text_emb, diagonal):
    logits = TEMP * jnp.dot(image_emb, text_emb.T, preferred_element_type=jnp.float32) + BIAS
    count = logits.shape[0]
    if diagonal:
        eye = lax.broadcasted_iota(jnp.int32, (count, count), 0) == lax.broadcasted_iota(jnp.int32, (count, count), 1)
        labels = jnp.where(eye, 1.0, -1.0).astype(jnp.float32)
    else:
        labels = -jnp.ones((count, count), jnp.float32)
    loss = lax.optimization_barrier(jnp.sum(-jax.nn.log_sigmoid(labels * logits), axis=1))
    weights = (-labels * jax.nn.sigmoid(-labels * logits) / count).astype(jnp.bfloat16)
    image_grad = TEMP * jnp.dot(weights, text_emb, preferred_element_type=jnp.float32)
    text_grad = TEMP * jnp.dot(weights.T, image_emb, preferred_element_type=jnp.float32)
    return (loss, image_grad, text_grad)

def head_back(feats, unit, norm, emb_grad):
    proj_grad = ((emb_grad - unit * lax.optimization_barrier(jnp.sum(unit * emb_grad, axis=1, keepdims=True))) / norm).astype(jnp.bfloat16)
    return lax.dot_general(feats, proj_grad, (((0,), (0,)), ((), ())), preferred_element_type=jnp.float32)

def reference(image_feats, text_feats, image_head, text_head):
    image_unit, image_norm = embed(image_feats, image_head)
    text_unit, text_norm = embed(text_feats, text_head)
    shape4 = (N_BLK, N_DP, ROWS, D)
    image_emb = image_unit.astype(jnp.bfloat16).reshape(shape4)
    text_emb = text_unit.astype(jnp.bfloat16).reshape(shape4)
    flat = (N_BLK * N_DP, ROWS, D)
    row_loss = jnp.zeros((N_BLK * N_DP, ROWS), jnp.float32)
    image_grad = jnp.zeros(flat, jnp.float32)
    text_grad = jnp.zeros(shape4, jnp.float32)
    for shift_by in range(3):
        texts = jnp.roll(text_emb, shift_by, axis=0).reshape(flat)
        diagonal = shift_by == 0
        loss, igrad, tgrad = lax.map(lambda pair: pair_terms(pair[0], pair[1], diagonal), (image_emb.reshape(flat), texts))
        row_loss = row_loss + loss
        image_grad = image_grad + igrad
        text_grad = text_grad + jnp.roll(tgrad.reshape(shape4), -shift_by, axis=0)
    total = N_BLK * N_DP * ROWS
    image_head_grad = head_back(image_feats, image_unit, image_norm, image_grad.reshape(total, D))
    text_head_grad = head_back(text_feats, text_unit, text_norm, text_grad.reshape(total, D))
    return (row_loss.reshape(total), image_head_grad, text_head_grad)
```

```python
import jax
import jax.numpy as jnp
from jax import lax
from jax.sharding import PartitionSpec as P

TEMP = 30.0
BIAS = -6.0
EPS = 1e-06
F32 = jnp.float32
BF16 = jnp.bfloat16


def embed(feats, head):
    proj = jnp.dot(feats, head, preferred_element_type=F32)
    norm = jnp.sqrt(jnp.sum(proj * proj, axis=1, keepdims=True) + EPS)
    return (proj / norm, norm)


def blk_move(value, even, odd):
    count = lax.axis_size("blk")
    pairs = [(k, (even(k) if k % 2 == 0 else odd(k)) % count) for k in range(count)]
    return lax.ppermute(value, "blk", pairs)


def other_core(value):
    count = lax.axis_size("dp")
    return lax.ppermute(value, "dp", [(k, k ^ 1) for k in range(count)])


def pair_weights(mine, theirs, diagonal):
    logits = TEMP * lax.dot_general(mine, theirs, (((1,), (1,)), ((), ())), preferred_element_type=F32) + BIAS
    count = logits.shape[0]
    if diagonal:
        eye = lax.broadcasted_iota(jnp.int32, logits.shape, 0) == lax.broadcasted_iota(jnp.int32, logits.shape, 1)
        labels = jnp.where(eye, 1.0, -1.0).astype(F32)
    else:
        labels = -jnp.ones(logits.shape, F32)
    loss = jnp.sum(-jax.nn.log_sigmoid(labels * logits), axis=1)
    weights = (-labels * jax.nn.sigmoid(-labels * logits) / count).astype(BF16)
    return loss, weights


def side(mine, partners):
    loss, grad = 0.0, 0.0
    for step, theirs in enumerate(partners):
        part, weights = pair_weights(mine, theirs, step == 0)
        loss = loss + part
        grad = grad + jnp.dot(weights, theirs, preferred_element_type=F32)
    return loss, TEMP * grad


def proj_grad(unit, norm, grad):
    return ((grad - unit * jnp.sum(unit * grad, axis=1, keepdims=True)) / norm).astype(BF16)


def row_dot(left, right):
    return lax.dot_general(left, right, (((0,), (0,)), ((), ())), preferred_element_type=F32)


def core_columns(feats, core):
    d = feats.shape[1]
    row = lax.broadcasted_iota(jnp.int32, (d, d // 2), 0)
    col = lax.broadcasted_iota(jnp.int32, (d, d // 2), 1)
    chosen = row == (col // 36) * 72 + core * 36 + col % 36
    return jnp.dot(feats, chosen.astype(BF16), preferred_element_type=F32).astype(BF16)


def body(image_feats, text_feats, image_head, text_head):
    even = lax.axis_index("blk") % 2 == 0
    core = lax.axis_index("dp") % 2
    image_unit, image_norm = embed(image_feats, image_head)
    text_unit, text_norm = embed(text_feats, text_head)

    def pick(x, y):
        return jnp.where(even, x, y)

    a_unit, b_unit = pick(text_unit, image_unit), pick(image_unit, text_unit)
    a_norm, b_norm = pick(text_norm, image_norm), pick(image_norm, text_norm)
    a_emb, b_emb = a_unit.astype(BF16), b_unit.astype(BF16)

    swap = (lambda k: k + 1, lambda k: k - 1)
    b_from = blk_move(b_emb, lambda k: k - 2, lambda k: k + 2)
    a_cross = blk_move(a_emb, *swap)
    a_from = blk_move(a_emb, lambda k: k + 2, lambda k: k - 2)
    b_cross = blk_move(b_from, *swap)

    a_feats = pick(text_feats, image_feats)
    b_feats = pick(image_feats, text_feats)
    a_own, b_own = core_columns(a_feats, core), core_columns(b_feats, core)
    a_oth = other_core(core_columns(a_feats, 1 - core))
    b_oth = other_core(core_columns(b_feats, 1 - core))

    def head_terms(unit, norm, grad, own, oth):
        mine = proj_grad(unit, norm, grad)
        theirs = other_core(mine)
        terms = (row_dot(mine, own) + row_dot(theirs, oth)).astype(BF16)
        terms = terms.reshape(8, 144, 576)
        return lax.all_to_all(terms, "blk", 0, 0)

    a_loss, a_grad = side(a_emb, (b_emb, a_cross, b_from))
    a_got = head_terms(a_unit, a_norm, a_grad, a_own, a_oth)
    b_loss, b_grad = side(b_emb, (a_emb, b_cross, a_from))
    b_got = head_terms(b_unit, b_norm, b_grad, b_own, b_oth)

    a_got = a_got.reshape(4, 2, 144, 576).astype(F32).sum(0)
    b_got = b_got.reshape(4, 2, 144, 576).astype(F32).sum(0)
    both = jnp.stack([a_got[1] + b_got[0], a_got[0] + b_got[1]])
    both = both.reshape(2, 144, 16, 36).transpose(2, 3, 0, 1).reshape(16, 36, 288)
    groups = [[2 * j + c for j in range(16)] for c in range(2)]
    both = lax.all_to_all(both, "dp", 0, 0, axis_index_groups=groups).sum(0)
    row_loss = pick(b_loss, a_loss)
    return row_loss, both[:, :144], both[:, 144:]


def solution(mesh):
    placed = (P(("blk", "dp"), None), P(("blk", "dp"), None), P(), P())
    return jax.shard_map(
        body,
        mesh=mesh,
        in_specs=placed,
        out_specs=(P(("blk", "dp")), P("dp", "blk"), P("dp", "blk")),
        check_vma=False,
    )
```

```python
import functools
import math

import jax
import jax.numpy as jnp
from jax import lax
from jax.experimental import pallas as pl
from jax.experimental.pallas import tpu as pltpu
from jax.sharding import Mesh
from jax.sharding import PartitionSpec as P

TEMP = 30.0
BIAS = -6.0
EPS = 1e-06
LOG2E = math.log2(math.e)
F32 = jnp.float32
BF16 = jnp.bfloat16
D = 1152
ROWS = 512
AXES = ("y", "xlo", "xhi", "z", "core")
SIZES = (4, 2, 2, 8, 2)
MIB = 1024 * 1024
EMBED_VMEM = 52
NT = (((1,), (1,)), ((), ()))

VMEM = functools.partial(pl.BlockSpec, memory_space=pltpu.VMEM)
SMEM = functools.partial(pl.BlockSpec, memory_space=pltpu.SMEM)
HBM = functools.partial(pl.BlockSpec, memory_space=pltpu.HBM)


def shape(dims, dtype):
    return jax.ShapeDtypeStruct(dims, dtype)


def call(kernel, name, ins, outs, out_specs=None, scratch=(), vmem=20):
    if out_specs is None:
        out_specs = jax.tree.map(lambda _: VMEM(), outs)
    return pl.pallas_call(
        kernel,
        name=name,
        in_specs=ins,
        out_shape=outs,
        out_specs=out_specs,
        scratch_shapes=list(scratch),
        compiler_params=pltpu.CompilerParams(vmem_limit_bytes=vmem * MIB),
        cost_estimate=pl.CostEstimate(flops=1000, bytes_accessed=1000, transcendentals=0),
    )


def embed_kernel(odd, image_feats, text_feats, image_head, text_head, *refs):
    outs, (feats, head, held, in_sems, out_sems) = refs[:6], refs[6:]
    cut = 3
    width = D // cut

    def loads(side, src_feats, src_head):
        yield pltpu.make_async_copy(src_feats, feats.at[side], in_sems.at[side, cut])
        for j in range(cut):
            cols = pl.ds(j * width, width)
            yield pltpu.make_async_copy(src_head.at[:, cols], head.at[side, :, cols], in_sems.at[side, j])

    for value in range(2):

        @pl.when(odd[0] == value)
        def _(value=value):
            order = ((text_feats, text_head), (image_feats, image_head))
            for side in range(2):
                for copy in loads(side, *order[side ^ value]):
                    copy.start()

    saves = []
    for side in range(2):
        emb, proj_out, norm = outs[3 * side : 3 * side + 3]
        waits = list(loads(side, image_feats, image_head))
        waits[0].wait()
        total = jnp.zeros((ROWS, 1), F32)
        for j in range(cut):
            cols = pl.ds(j * width, width)
            waits[j + 1].wait()
            proj = jnp.dot(feats[side], head[side, :, cols], preferred_element_type=F32)
            held[side, :, cols] = proj
            saves.append(pltpu.make_async_copy(held.at[side, :, cols], proj_out.at[:, cols], out_sems.at[side, j]))
            saves[-1].start()
            total += jnp.sum(proj * proj, axis=1, keepdims=True)
        length = jnp.sqrt(total + EPS)
        norm[...] = length
        emb[...] = (held[side] * (1.0 / length)).astype(BF16)
    for copy in saves:
        copy.wait()


def embed(odd, image_feats, text_feats, image_head, text_head):
    one = [shape((ROWS, D), BF16), shape((ROWS, D), F32), shape((ROWS, 1), F32)]
    return call(
        embed_kernel,
        "embed",
        [SMEM(), HBM(), HBM(), HBM(), HBM()],
        one + one,
        out_specs=[VMEM(), HBM(), VMEM()] * 2,
        scratch=[
            pltpu.VMEM((2, ROWS, D), BF16),
            pltpu.VMEM((2, D, D), BF16),
            pltpu.VMEM((2, ROWS, D), F32),
            pltpu.SemaphoreType.DMA((2, 4)),
            pltpu.SemaphoreType.DMA((2, 3)),
        ],
        vmem=EMBED_VMEM,
    )(odd, image_feats, text_feats, image_head, text_head)


def add_pair(mine, theirs, rows, diagonal):
    dots = lax.dot_general(mine[rows, :], theirs[...], NT, preferred_element_type=F32)
    grow = dots * (-TEMP * LOG2E) + (-BIAS * LOG2E)
    if diagonal:
        row = lax.broadcasted_iota(jnp.int32, dots.shape, 0) + rows.start
        eye = row == lax.broadcasted_iota(jnp.int32, dots.shape, 1)
        grow = jnp.where(eye, -grow, grow)
    weights = 1.0 / (float(ROWS) + jnp.exp2(grow + math.log2(ROWS)))
    if diagonal:
        weights = jnp.where(eye, -weights, weights)
    return jnp.dot(weights.astype(BF16), theirs[...], preferred_element_type=F32)


def side_kernel(count, diagonal, last, *refs):
    mine, partners, rest = refs[0], refs[1 : 1 + count], refs[1 + count :]
    if last:
        before, proj, norm, out = rest
    else:
        (out,) = rest
    block = 256
    for i in range(ROWS // block):
        rows = pl.ds(i * block, block)
        grad = before[rows, :] if last else None
        for step, theirs in enumerate(partners):
            part = add_pair(mine, theirs, rows, diagonal and step == 0)
            grad = part if grad is None else grad + part
        if last:
            grad = TEMP * grad
            inverse = 1.0 / norm[rows, :]
            own = proj[rows, :] * inverse
            along = jnp.sum(own * grad, axis=1, keepdims=True)
            value = (grad - own * along) * inverse
            out[:, rows] = value.T.astype(BF16)
        else:
            out[rows, :] = grad


def side(mine, partners, diagonal, before=None, proj=None, norm=None):
    last = before is not None
    args = [mine, *partners] + ([before, proj, norm] if last else [])
    return call(
        functools.partial(side_kernel, len(partners), diagonal, last),
        "side_last" if last else "side_first",
        [VMEM()] * len(args),
        shape((D, ROWS), BF16) if last else shape((ROWS, D), F32),
    )(*args)


def loss_kernel(use_a, a_emb, b_emb, a_cross, b_cross, a_from, b_from, out):
    def total(mine, partners):
        result = jnp.zeros((1, ROWS), F32)
        for step, theirs in enumerate(partners):
            for i in range(2):
                rows = pl.ds(i * 256, 256)
                z = TEMP * lax.dot_general(theirs[rows, :], mine[...], NT, preferred_element_type=F32) + BIAS
                if step == 0:
                    row = lax.broadcasted_iota(jnp.int32, z.shape, 0) + i * 256
                    z = jnp.where(row == lax.broadcasted_iota(jnp.int32, z.shape, 1), -z, z)
                soft = jnp.maximum(z, 0.0) + jnp.log1p(jnp.exp(-jnp.abs(z)))
                result += jnp.sum(soft, axis=0, keepdims=True)
        out[...] = result

    @pl.when(use_a[0] == 1)
    def _():
        total(a_emb, (b_emb, a_cross, b_from))

    @pl.when(use_a[0] != 1)
    def _():
        total(b_emb, (a_emb, b_cross, a_from))


def head_own_kernel(grad, feats, out):
    out[...] = jnp.dot(grad[...], feats[...], preferred_element_type=F32)


def head_pack_kernel(grad, feats, before, out):
    for y in range(4):
        rows = pl.ds(y * 288, 288)
        terms = before[rows, :] + jnp.dot(grad[rows, :], feats[...], preferred_element_type=F32)
        for xhi in range(2):
            base = xhi * 384
            chunk = 2 * y + xhi
            out[chunk, 0:288, :] = terms[:, base : base + 128].astype(BF16)
            out[chunk, 288:576, :] = terms[:, base + 128 : base + 256].astype(BF16)
            few = terms[:, base + 256 : base + 384]
            few = few[0:96] + pltpu.roll(few[96:192], 32, 1) + pltpu.roll(few[192:288], 64, 1)
            out[chunk, 576:672, :] = few.astype(BF16)


def repack(total, store):
    lane = lax.broadcasted_iota(jnp.int32, (48, 128), 1)
    for z in range(8):
        for xlo in range(2):
            value = jnp.zeros((48, 128), F32)
            for g in range(3):
                m = xlo * 144 + g * 48
                wide = total[(z // 4) * 288 + m : (z // 4) * 288 + m + 48, :]
                move = (32 * g - 32 * (z % 4)) % 128
                wide = pltpu.roll(wide, move, 1) if move else wide
                value = jnp.where((lane >= 32 * g) & (lane < 32 * g + 32), wide, value)
                group, row = m // 96, m % 96
                few = total[576 + row : 576 + row + 48, :]
                move = (96 + 4 * g - 32 * group - 4 * z) % 128
                few = pltpu.roll(few, move, 1) if move else few
                first = 96 + 4 * g
                value = jnp.where((lane >= first) & (lane < first + 4), few, value)
            store(z, xlo, value)


def add_y_kernel(xhi, got, keep, give):
    def total(which):
        value = got[0, which].astype(F32)
        for s in range(1, 4):
            value = value + got[s, which].astype(F32)
        return value

    keep[...] = total(xhi[0])
    give[...] = total(1 - xhi[0]).astype(BF16)


def add_pack_kernel(a_keep, a_take, b_got, out):
    a_total = a_keep[...] + a_take[...].astype(F32)
    b_total = b_got[0].astype(F32)
    for s in range(1, 8):
        b_total = b_total + b_got[s].astype(F32)
    for side, total in enumerate((a_total, b_total)):

        def store(z, xlo, value, side=side):
            out[z, xlo, side] = value.astype(BF16)

        repack(total, store)


def finish_kernel(got, image, text):
    for out, parity in ((text, 0), (image, 1)):
        value = jnp.zeros((48, 128), F32)
        for z in range(8):
            value = value + got[z, parity, 0].astype(F32) + got[z, 1 - parity, 1].astype(F32)
        turned = value.T
        parts = []
        for g in range(3):
            parts.append(jnp.concatenate([turned[32 * g : 32 * g + 32], turned[96 + 4 * g : 100 + 4 * g]], axis=0))
        out[...] = jnp.concatenate(parts, axis=1)


def position(coords):
    index = 0
    for coord, size in zip(coords, SIZES):
        index = index * size + coord % size
    return index


def move(value, target):
    pairs = []
    for source in range(math.prod(SIZES)):
        rest, coords = source, []
        for size in reversed(SIZES):
            coords.insert(0, rest % size)
            rest //= size
        pairs.append((source, position(target(*coords))))
    return lax.ppermute(value, AXES, pairs)


def swap_x(value):
    return move(value, lambda y, xl, xh, z, c: (y, 1 - xl, xh, z, c))


def swap_core(value):
    return move(value, lambda y, xl, xh, z, c: (y, xl, xh, z, 1 - c))


def shift_y(value, even, odd):
    return move(value, lambda y, xl, xh, z, c: (y + (odd if xl else even), xl, xh, z, c))


def after(values, *earlier):
    return lax.optimization_barrier((*values, *earlier))[: len(values)]


def core_columns(core):
    row = lax.broadcasted_iota(jnp.int32, (D, 768), 0)
    col = lax.broadcasted_iota(jnp.int32, (D, 768), 1)
    xhi, lane = col // 384, col % 384
    few = lane >= 256
    z = jnp.where(few, (lane - 256) // 4, lane // 32)
    r = jnp.where(few, 32 + (lane - 256) % 4, lane % 32)
    source = jnp.where(lane < 288, xhi * 576 + z * 72 + core * 36 + r, -1)
    return (row == source).astype(BF16)


def body(image_feats, text_feats, image_head, text_head):
    odd = lax.axis_index("xlo")
    core = lax.axis_index("core")
    flag = odd.astype(jnp.int32).reshape(1)

    a_emb, a_proj, a_norm, b_emb, b_proj, b_norm = embed(flag, image_feats, text_feats, image_head, text_head)
    a_cross = swap_x(a_emb)
    b_from = shift_y(b_emb, -1, 1)
    a_from = shift_y(a_emb, 1, -1)

    def together(steps, *args):
        def nothing(*_):
            return jax.tree.map(lambda x: jnp.zeros(x.shape, x.dtype), jax.eval_shape(steps, *args))

        return lax.cond(flag[0] < 2, steps, nothing, *args)

    def prepare(image_feats, text_feats, a_emb, b_emb):
        own_columns, oth_columns = core_columns(core), core_columns(1 - core)
        a_feats = jnp.where(odd == 1, image_feats, text_feats)
        b_feats = jnp.where(odd == 1, text_feats, image_feats)

        def columns(feats):
            own = jnp.dot(feats, own_columns, preferred_element_type=F32).astype(BF16)
            oth = jnp.dot(feats, oth_columns, preferred_element_type=F32).astype(BF16)
            return own, swap_core(oth)

        return (*columns(a_feats), *columns(b_feats), side(a_emb, (b_emb,), True))

    a_own, a_oth, b_own, b_oth, a_first = together(prepare, image_feats, text_feats, a_emb, b_emb)
    b_from, a_from = after((b_from, a_from), a_own, b_own, a_oth, b_oth, a_first)
    b_cross = swap_x(b_from)

    def head_terms(mine, own, oth):
        theirs = swap_core(mine)
        before = call(head_own_kernel, "head_own", [VMEM()] * 2, shape((D, 768), F32))(mine, own)
        return call(head_pack_kernel, "head_pack", [VMEM()] * 3, shape((8, 672, 128), BF16))(theirs, oth, before)

    def finished(mine, partners, before, proj, norm, own, oth):
        return head_terms(side(mine, partners, False, before, proj, norm), own, oth)

    a_terms = together(finished, a_emb, (a_cross, b_from), a_first, a_proj, a_norm, a_own, a_oth)
    a_got = lax.all_to_all(a_terms.reshape(4, 2, 672, 128), "y", 0, 0)

    (a_from,) = after((a_from,), a_terms)
    b_first = side(b_emb, (a_emb, a_from), True)
    a_keep, a_give = call(
        add_y_kernel, "add_y", [SMEM(), VMEM()], [shape((672, 128), F32), shape((672, 128), BF16)]
    )(lax.axis_index("xhi").astype(jnp.int32).reshape(1), a_got)
    a_take = move(a_give, lambda y, xl, xh, z, c: (y, xl, 1 - xh, z, c))

    (b_cross,) = after((b_cross,), b_first)
    b_terms = together(finished, b_emb, (b_cross,), b_first, b_proj, b_norm, b_own, b_oth)
    b_got = lax.all_to_all(b_terms, ("y", "xhi"), 0, 0)

    (loss_emb,) = after((a_emb,), b_terms)
    row_loss = call(loss_kernel, "loss", [SMEM()] + [VMEM()] * 6, shape((1, ROWS), F32))(
        flag, loss_emb, b_emb, a_cross, b_cross, a_from, b_from
    )
    (b_got,) = after((b_got,), row_loss)
    part = call(add_pack_kernel, "add_pack", [VMEM()] * 3, shape((8, 2, 2, 48, 128), BF16))(a_keep, a_take, b_got)
    got = lax.all_to_all(part.reshape(16, 2, 48, 128), ("z", "xlo"), 0, 0).reshape(8, 2, 2, 48, 128)
    image_grad, text_grad = call(
        finish_kernel, "finish", [VMEM()], [shape((36, 144), F32), shape((36, 144), F32)]
    )(got)
    return row_loss.reshape(ROWS), image_grad, text_grad


def solution(mesh):
    fine = Mesh(mesh.devices.reshape(SIZES), AXES)
    blk, dp = ("y", "xlo"), ("xhi", "z", "core")
    placed = (P(AXES, None), P(AXES, None), P(), P())
    return jax.shard_map(
        body,
        mesh=fine,
        in_specs=placed,
        out_specs=(P(AXES), P(dp, blk), P(dp, blk)),
        check_vma=False,
    )
```

```python
import functools
import math

import jax
import jax.numpy as jnp
from jax import lax
from jax.experimental import pallas as pl
from jax.experimental.pallas import tpu as pltpu
from jax.sharding import Mesh
from jax.sharding import PartitionSpec as P

TEMP = 30.0
BIAS = -6.0
EPS = 1e-06
LOG2E = math.log2(math.e)
F32 = jnp.float32
BF16 = jnp.bfloat16
D = 1152
ROWS = 512
AXES = ("y", "xlo", "xhi", "z", "core")
SIZES = (4, 2, 2, 8, 2)
MIB = 1024 * 1024
EMBED_VMEM = 52
NT = (((1,), (1,)), ((), ()))

VMEM = functools.partial(pl.BlockSpec, memory_space=pltpu.VMEM)
SMEM = functools.partial(pl.BlockSpec, memory_space=pltpu.SMEM)
HBM = functools.partial(pl.BlockSpec, memory_space=pltpu.HBM)


def shape(dims, dtype):
    return jax.ShapeDtypeStruct(dims, dtype)


def call(kernel, name, ins, outs, out_specs=None, scratch=(), vmem=20):
    if out_specs is None:
        out_specs = jax.tree.map(lambda _: VMEM(), outs)
    return pl.pallas_call(
        kernel,
        name=name,
        in_specs=ins,
        out_shape=outs,
        out_specs=out_specs,
        scratch_shapes=list(scratch),
        compiler_params=pltpu.CompilerParams(vmem_limit_bytes=vmem * MIB),
        cost_estimate=pl.CostEstimate(flops=1000, bytes_accessed=1000, transcendentals=0),
    )


def embed_kernel(odd, image_feats, text_feats, image_head, text_head, *refs):
    outs, (feats, head, held, in_sems, out_sems) = refs[:6], refs[6:]
    cuts = (pl.ds(0, 512), pl.ds(512, 512), pl.ds(1024, 128))

    def loads(side, src_feats, src_head):
        yield pltpu.make_async_copy(src_feats, feats.at[side], in_sems.at[side, 3])
        for j, cols in enumerate(cuts):
            yield pltpu.make_async_copy(src_head.at[:, cols], head.at[side, :, cols], in_sems.at[side, j])

    for value in range(2):

        @pl.when(odd[0] == value)
        def _(value=value):
            order = ((text_feats, text_head), (image_feats, image_head))
            for side in range(2):
                for copy in loads(side, *order[side ^ value]):
                    copy.start()

    saves = []
    for side in range(2):
        emb, proj_out, norm = outs[3 * side : 3 * side + 3]
        waits = list(loads(side, image_feats, image_head))
        waits[0].wait()
        total = jnp.zeros((ROWS, 1), F32)
        for j, cols in enumerate(cuts):
            waits[j + 1].wait()
            proj = jnp.dot(feats[side], head[side, :, cols], preferred_element_type=F32)
            held[side, :, cols] = proj
            saves.append(pltpu.make_async_copy(held.at[side, :, cols], proj_out.at[:, cols], out_sems.at[side, j]))
            saves[-1].start()
            total += jnp.sum(proj * proj, axis=1, keepdims=True)
        length = jnp.sqrt(total + EPS)
        norm[...] = length
        emb[...] = (held[side] * (1.0 / length)).astype(BF16)
    for copy in saves:
        copy.wait()


def embed(odd, image_feats, text_feats, image_head, text_head):
    one = [shape((ROWS, D), BF16), shape((ROWS, D), F32), shape((ROWS, 1), F32)]
    return call(
        embed_kernel,
        "embed",
        [SMEM(), HBM(), HBM(), HBM(), HBM()],
        one + one,
        out_specs=[VMEM(), HBM(), VMEM()] * 2,
        scratch=[
            pltpu.VMEM((2, ROWS, D), BF16),
            pltpu.VMEM((2, D, D), BF16),
            pltpu.VMEM((2, ROWS, D), F32),
            pltpu.SemaphoreType.DMA((2, 4)),
            pltpu.SemaphoreType.DMA((2, 3)),
        ],
        vmem=EMBED_VMEM,
    )(odd, image_feats, text_feats, image_head, text_head)


def add_pair(mine, theirs, rows, diagonal):
    dots = lax.dot_general(mine[rows, :], theirs[...], NT, preferred_element_type=F32)
    grow = dots * (-TEMP * LOG2E) + (-BIAS * LOG2E)
    if diagonal:
        row = lax.broadcasted_iota(jnp.int32, dots.shape, 0) + rows.start
        eye = row == lax.broadcasted_iota(jnp.int32, dots.shape, 1)
        grow = jnp.where(eye, -grow, grow)
    weights = 1.0 / (float(ROWS) + jnp.exp2(grow + math.log2(ROWS)))
    if diagonal:
        weights = jnp.where(eye, -weights, weights)
    return jnp.dot(weights.astype(BF16), theirs[...], preferred_element_type=F32)


def side_kernel(count, diagonal, adds, last, *refs):
    refs = list(refs)
    take = lambda number: [refs.pop(0) for _ in range(number)]
    sources = take(1 + count + adds + last)
    norm = take(1)[0] if last else None
    (out,) = take(1)
    bufs = take(len(sources))
    held = None if last else take(1)[0]
    in_sems, out_sems = refs
    block = 256
    parts = [pl.ds(i * block, block) for i in range(ROWS // block)]
    loads = {}
    for k in range(1 + count):
        loads[k] = pltpu.make_async_copy(sources[k], bufs[k], in_sems.at[k, 0])
        loads[k].start()
    for i, rows in enumerate(parts):
        for k in range(1 + count, len(sources)):
            loads[k, i] = pltpu.make_async_copy(sources[k].at[rows, :], bufs[k].at[rows, :], in_sems.at[k, i])
            loads[k, i].start()
    saves = []
    loads[0].wait()
    for i, rows in enumerate(parts):
        grad = None
        for step in range(count):
            if i == 0:
                loads[1 + step].wait()
            part = add_pair(bufs[0], bufs[1 + step], rows, diagonal and step == 0)
            grad = part if grad is None else grad + part
        if adds:
            loads[1 + count, i].wait()
            grad = grad + bufs[1 + count][rows, :]
        if last:
            loads[1 + count + adds, i].wait()
            grad = TEMP * grad
            inverse = 1.0 / norm[rows, :]
            own = bufs[1 + count + adds][rows, :] * inverse
            along = jnp.sum(own * grad, axis=1, keepdims=True)
            value = (grad - own * along) * inverse
            out[:, rows] = value.astype(BF16).T
        else:
            held[rows, :] = grad
            saves.append(pltpu.make_async_copy(held.at[rows, :], out.at[rows, :], out_sems.at[i]))
            saves[-1].start()
    for copy in saves:
        copy.wait()


def side(mine, partners, diagonal, before=None, proj=None, norm=None):
    last = proj is not None
    adds = before is not None
    args = [mine, *partners] + [before] * adds + [proj] * last
    wide = pltpu.VMEM((ROWS, D), F32)
    scratch = [pltpu.VMEM((ROWS, D), BF16)] * (1 + len(partners)) + [wide] * (adds + last) + [wide] * (not last)
    scratch += [pltpu.SemaphoreType.DMA((len(args), 2)), pltpu.SemaphoreType.DMA((2,))]
    return call(
        functools.partial(side_kernel, len(partners), diagonal, adds, last),
        "side_last" if last else "side_first",
        [HBM()] * len(args) + [VMEM()] * last,
        shape((D, ROWS), BF16) if last else shape((ROWS, D), F32),
        out_specs=VMEM() if last else HBM(),
        scratch=scratch,
        vmem=24,
    )(*args, *([norm] * last))


def loss_kernel(use_a, a_emb, b_emb, a_cross, b_cross, a_from, b_from, out):
    def total(mine, partners):
        result = jnp.zeros((1, ROWS), F32)
        for step, theirs in enumerate(partners):
            for i in range(2):
                rows = pl.ds(i * 256, 256)
                z = TEMP * lax.dot_general(theirs[rows, :], mine[...], NT, preferred_element_type=F32) + BIAS
                if step == 0:
                    row = lax.broadcasted_iota(jnp.int32, z.shape, 0) + i * 256
                    z = jnp.where(row == lax.broadcasted_iota(jnp.int32, z.shape, 1), -z, z)
                soft = jnp.maximum(z, 0.0) + jnp.log1p(jnp.exp(-jnp.abs(z)))
                result += jnp.sum(soft, axis=0, keepdims=True)
        out[...] = result

    @pl.when(use_a[0] == 1)
    def _():
        total(a_emb, (b_emb, a_cross, b_from))

    @pl.when(use_a[0] != 1)
    def _():
        total(b_emb, (a_emb, b_cross, a_from))


def head_own_kernel(grad, feats, out):
    out[...] = jnp.dot(grad[...], feats[...], preferred_element_type=F32)


def head_pack_kernel(grad, feats, before, out, held, sems):
    copies = []
    for y in range(4):
        rows = pl.ds(y * 288, 288)
        terms = before[rows, :] + jnp.dot(grad[rows, :], feats[...], preferred_element_type=F32)
        for xlo in range(2):
            for xhi in range(2):
                some = terms[xlo * 144 : xlo * 144 + 144, xhi * 384 : xhi * 384 + 384]
                chunk = 4 * y + 2 * xlo + xhi
                held[chunk, 0:144, :] = some[:, 0:128].astype(BF16)
                held[chunk, 144:288, :] = some[:, 128:256].astype(BF16)
                few = some[:, 256:384]
                few = few[0:48] + pltpu.roll(few[48:96], 32, 1) + pltpu.roll(few[96:144], 64, 1)
                held[chunk, 288:336, :] = few.astype(BF16)
        four = pl.ds(4 * y, 4)
        copies.append(pltpu.make_async_copy(held.at[four], out.at[four], sems.at[y]))
        copies[-1].start()
    for copy in copies:
        copy.wait()


def repack(total, store):
    lane = lax.broadcasted_iota(jnp.int32, (48, 128), 1)
    for z in range(8):
        value = jnp.zeros((48, 128), F32)
        for g in range(3):
            first = (z // 4) * 144 + g * 48
            wide = total[first : first + 48, :]
            turn = (32 * g - 32 * (z % 4)) % 128
            wide = pltpu.roll(wide, turn, 1) if turn else wide
            value = jnp.where((lane >= 32 * g) & (lane < 32 * g + 32), wide, value)
            few = total[288:336, :]
            turn = (96 + 4 * g - 32 * g - 4 * z) % 128
            few = pltpu.roll(few, turn, 1) if turn else few
            first = 96 + 4 * g
            value = jnp.where((lane >= first) & (lane < first + 4), few, value)
        store(z, value)


def add_y_kernel(me, got, *outs):
    for far, out in enumerate(outs):
        which = me[0] ^ far
        value = got[0, which].astype(F32)
        for s in range(1, 4):
            value = value + got[s, which].astype(F32)
        out[...] = value.astype(out.dtype)


def add_pack_kernel(odd, keep, near, cross, corner, b_got, out):
    same = keep[...] + near[...].astype(F32)
    other = cross[...].astype(F32) + corner[...].astype(F32)
    is_odd = odd[0] == 1
    for head in range(2):
        total = jnp.where(is_odd, other, same) if head == 0 else jnp.where(is_odd, same, other)
        for y in range(4):
            for xhi in range(2):
                total = total + b_got[4 * y + 2 * (1 - head) + xhi].astype(F32)

        def store(z, value, head=head):
            out[z, head] = value

        repack(total, store)


def finish_kernel(got, text, image):
    for head, out in enumerate((text, image)):
        turned = jnp.sum(got[:, head], axis=0).T
        parts = []
        for g in range(3):
            parts.append(jnp.concatenate([turned[32 * g : 32 * g + 32], turned[96 + 4 * g : 100 + 4 * g]], axis=0))
        out[...] = jnp.concatenate(parts, axis=1)


def position(coords):
    index = 0
    for coord, size in zip(coords, SIZES):
        index = index * size + coord % size
    return index


def move(value, target):
    pairs = []
    for source in range(math.prod(SIZES)):
        rest, coords = source, []
        for size in reversed(SIZES):
            coords.insert(0, rest % size)
            rest //= size
        pairs.append((source, position(target(*coords))))
    return lax.ppermute(value, AXES, pairs)


def swap_x(value):
    return move(value, lambda y, xl, xh, z, c: (y, 1 - xl, xh, z, c))


def swap_core(value):
    return move(value, lambda y, xl, xh, z, c: (y, xl, xh, z, 1 - c))


def shift_y(value, even, odd):
    return move(value, lambda y, xl, xh, z, c: (y + (odd if xl else even), xl, xh, z, c))


def after(values, *earlier):
    return lax.optimization_barrier((*values, *earlier))[: len(values)]


def core_columns(core):
    row = lax.broadcasted_iota(jnp.int32, (D, 768), 0)
    col = lax.broadcasted_iota(jnp.int32, (D, 768), 1)
    xhi, lane = col // 384, col % 384
    few = lane >= 256
    z = jnp.where(few, (lane - 256) // 4, lane // 32)
    r = jnp.where(few, 32 + (lane - 256) % 4, lane % 32)
    source = jnp.where(lane < 288, xhi * 576 + z * 72 + core * 36 + r, -1)
    return (row == source).astype(BF16)


def body(image_feats, text_feats, image_head, text_head):
    odd = lax.axis_index("xlo")
    core = lax.axis_index("core")
    flag = odd.astype(jnp.int32).reshape(1)

    a_emb, a_proj, a_norm, b_emb, b_proj, b_norm = embed(flag, image_feats, text_feats, image_head, text_head)
    a_cross = swap_x(a_emb)
    b_from = shift_y(b_emb, -1, 1)
    a_from = shift_y(a_emb, 1, -1)

    def together(steps, *args):
        def nothing(*_):
            return jax.tree.map(lambda x: jnp.zeros(x.shape, x.dtype), jax.eval_shape(steps, *args))

        return lax.cond(flag[0] < 2, steps, nothing, *args)

    def prepare(image_feats, text_feats, a_emb, b_emb):
        own_columns, oth_columns = core_columns(core), core_columns(1 - core)
        a_feats = jnp.where(odd == 1, image_feats, text_feats)
        b_feats = jnp.where(odd == 1, text_feats, image_feats)

        def columns(feats):
            own = jnp.dot(feats, own_columns, preferred_element_type=F32).astype(BF16)
            oth = jnp.dot(feats, oth_columns, preferred_element_type=F32).astype(BF16)
            return own, swap_core(oth)

        firsts = side(a_emb, (b_emb,), True), side(b_emb, (a_emb,), True)
        return (*columns(a_feats), *columns(b_feats), *firsts)

    a_own, a_oth, b_own, b_oth, a_first, b_first = together(prepare, image_feats, text_feats, a_emb, b_emb)
    (a_cross,) = after((a_cross,), a_own, b_own, a_oth, b_oth, a_first, b_first)
    (b_from,) = after((b_from,), a_cross)
    b_cross = swap_x(b_from)
    (a_first,) = after((a_first,), a_from)

    def head_terms(mine, own, oth):
        theirs = swap_core(mine)
        before = call(head_own_kernel, "head_own", [VMEM()] * 2, shape((D, 768), F32))(mine, own)
        return call(
            head_pack_kernel,
            "head_pack",
            [VMEM()] * 3,
            shape((16, 336, 128), BF16),
            out_specs=HBM(),
            scratch=[pltpu.VMEM((16, 336, 128), BF16), pltpu.SemaphoreType.DMA((4,))],
        )(theirs, oth, before)

    def finished(mine, partners, before, proj, norm, own, oth):
        return head_terms(side(mine, partners, False, before, proj, norm), own, oth)

    a_terms = together(finished, a_emb, (a_cross, b_from), a_first, a_proj, a_norm, a_own, a_oth)
    a_got = lax.all_to_all(a_terms.reshape(4, 4, 336, 128), "y", 0, 0)
    me = (2 * odd + lax.axis_index("xhi")).astype(jnp.int32).reshape(1)
    keep, near, cross, corner = call(add_y_kernel, "add_y", [SMEM(), VMEM()], [shape((336, 128), F32)] + [shape((336, 128), BF16)] * 3)(
        me, a_got
    )
    near = move(near, lambda y, xl, xh, z, c: (y, xl, 1 - xh, z, c))
    cross = move(cross, lambda y, xl, xh, z, c: (y, 1 - xl, xh, z, c))
    corner = move(corner, lambda y, xl, xh, z, c: (y, 1 - xl, 1 - xh, z, c))

    (a_from,) = after((a_from,), a_terms)
    b_first = side(b_emb, (a_from,), False, b_first)
    b_terms = together(finished, b_emb, (b_cross,), b_first, b_proj, b_norm, b_own, b_oth)
    b_got = lax.all_to_all(b_terms, ("y", "xlo", "xhi"), 0, 0)

    (loss_emb,) = after((a_emb,), b_terms)
    row_loss = call(loss_kernel, "loss", [SMEM()] + [VMEM()] * 6, shape((1, ROWS), F32))(
        flag, loss_emb, b_emb, a_cross, b_cross, a_from, b_from
    )
    (b_got,) = after((b_got,), row_loss)
    part = call(add_pack_kernel, "add_pack", [SMEM()] + [VMEM()] * 5, shape((8, 2, 48, 128), F32))(
        flag, keep, near, cross, corner, b_got
    )
    got = lax.all_to_all(part, "z", 0, 0)
    text_grad, image_grad = call(finish_kernel, "finish", [VMEM()], [shape((36, 144), F32), shape((36, 144), F32)])(got)
    return row_loss.reshape(ROWS), image_grad, text_grad


def solution(mesh):
    fine = Mesh(mesh.devices.reshape(SIZES), AXES)
    blk, dp = ("y", "xlo"), ("xhi", "z", "core")
    placed = (P(AXES, None), P(AXES, None), P(), P())
    return jax.shard_map(
        body,
        mesh=fine,
        in_specs=placed,
        out_specs=(P(AXES), P(dp, blk), P(dp, blk)),
        check_vma=False,
    )
```

```python
import functools
import math

import jax
import jax.numpy as jnp
from jax import lax
from jax.experimental import pallas as pl
from jax.experimental.pallas import tpu as pltpu
from jax.sharding import Mesh
from jax.sharding import PartitionSpec as P

TEMP = 30.0
BIAS = -6.0
EPS = 1e-06
LOG2E = math.log2(math.e)
F32 = jnp.float32
BF16 = jnp.bfloat16
D = 1152
ROWS = 512
AXES = ("y", "xlo", "xhi", "z", "core")
SIZES = (4, 2, 2, 8, 2)
MIB = 1024 * 1024
EMBED_VMEM = 52
NT = (((1,), (1,)), ((), ()))

VMEM = functools.partial(pl.BlockSpec, memory_space=pltpu.VMEM)
SMEM = functools.partial(pl.BlockSpec, memory_space=pltpu.SMEM)
HBM = functools.partial(pl.BlockSpec, memory_space=pltpu.HBM)


def shape(dims, dtype):
    return jax.ShapeDtypeStruct(dims, dtype)


def call(kernel, name, ins, outs, out_specs=None, scratch=(), vmem=20):
    if out_specs is None:
        out_specs = jax.tree.map(lambda _: VMEM(), outs)
    return pl.pallas_call(
        kernel,
        name=name,
        in_specs=ins,
        out_shape=outs,
        out_specs=out_specs,
        scratch_shapes=list(scratch),
        compiler_params=pltpu.CompilerParams(vmem_limit_bytes=vmem * MIB),
        cost_estimate=pl.CostEstimate(flops=1000, bytes_accessed=1000, transcendentals=0),
    )


def embed_kernel(odd, image_feats, text_feats, image_head, text_head, *refs):
    outs, (feats, head, held, in_sems, out_sems) = refs[:6], refs[6:]
    cuts = (pl.ds(0, 512), pl.ds(512, 512), pl.ds(1024, 128))

    def loads(side, src_feats, src_head):
        yield pltpu.make_async_copy(src_feats, feats.at[side], in_sems.at[side, 3])
        for j, cols in enumerate(cuts):
            yield pltpu.make_async_copy(src_head.at[:, cols], head.at[side, :, cols], in_sems.at[side, j])

    for value in range(2):

        @pl.when(odd[0] == value)
        def _(value=value):
            order = ((text_feats, text_head), (image_feats, image_head))
            for side in range(2):
                for copy in loads(side, *order[side ^ value]):
                    copy.start()

    saves = []
    for side in range(2):
        emb, proj_out, norm = outs[3 * side : 3 * side + 3]
        waits = list(loads(side, image_feats, image_head))
        waits[0].wait()
        total = jnp.zeros((ROWS, 1), F32)
        for j, cols in enumerate(cuts):
            waits[j + 1].wait()
            proj = jnp.dot(feats[side], head[side, :, cols], preferred_element_type=F32)
            held[side, :, cols] = proj
            saves.append(pltpu.make_async_copy(held.at[side, :, cols], proj_out.at[:, cols], out_sems.at[side, j]))
            saves[-1].start()
            total += jnp.sum(proj * proj, axis=1, keepdims=True)
        length = jnp.sqrt(total + EPS)
        norm[...] = length
        emb[...] = (held[side] * (1.0 / length)).astype(BF16)
    for copy in saves:
        copy.wait()


def embed(odd, image_feats, text_feats, image_head, text_head):
    one = [shape((ROWS, D), BF16), shape((ROWS, D), F32), shape((ROWS, 1), F32)]
    return call(
        embed_kernel,
        "embed",
        [SMEM(), HBM(), HBM(), HBM(), HBM()],
        one + one,
        out_specs=[VMEM(), HBM(), VMEM()] * 2,
        scratch=[
            pltpu.VMEM((2, ROWS, D), BF16),
            pltpu.VMEM((2, D, D), BF16),
            pltpu.VMEM((2, ROWS, D), F32),
            pltpu.SemaphoreType.DMA((2, 4)),
            pltpu.SemaphoreType.DMA((2, 3)),
        ],
        vmem=EMBED_VMEM,
    )(odd, image_feats, text_feats, image_head, text_head)


def add_pair(mine, theirs, rows, diagonal):
    dots = lax.dot_general(mine[rows, :], theirs[...], NT, preferred_element_type=F32)
    grow = dots * (-TEMP * LOG2E) + (-BIAS * LOG2E)
    if diagonal:
        row = lax.broadcasted_iota(jnp.int32, dots.shape, 0) + rows.start
        eye = row == lax.broadcasted_iota(jnp.int32, dots.shape, 1)
        grow = jnp.where(eye, -grow, grow)
    weights = 1.0 / (float(ROWS) + jnp.exp2(grow + math.log2(ROWS)))
    if diagonal:
        weights = jnp.where(eye, -weights, weights)
    return jnp.dot(weights.astype(BF16), theirs[...], preferred_element_type=F32)


def side_kernel(count, diagonal, adds, last, *refs):
    refs = list(refs)
    take = lambda number: [refs.pop(0) for _ in range(number)]
    sources = take(1 + count + adds + last)
    norm = take(1)[0] if last else None
    (out,) = take(1)
    bufs = take(len(sources))
    held = None if last else take(1)[0]
    in_sems, out_sems = refs
    block = 512
    parts = [pl.ds(i * block, block) for i in range(ROWS // block)]
    loads = {}
    for k in range(1 + count):
        loads[k] = pltpu.make_async_copy(sources[k], bufs[k], in_sems.at[k, 0])
        loads[k].start()
    for i, rows in enumerate(parts):
        for k in range(1 + count, len(sources)):
            loads[k, i] = pltpu.make_async_copy(sources[k].at[rows, :], bufs[k].at[rows, :], in_sems.at[k, i])
            loads[k, i].start()
    saves = []
    loads[0].wait()
    for i, rows in enumerate(parts):
        grad = None
        for step in range(count):
            if i == 0:
                loads[1 + step].wait()
            part = add_pair(bufs[0], bufs[1 + step], rows, diagonal and step == 0)
            grad = part if grad is None else grad + part
        if adds:
            loads[1 + count, i].wait()
            grad = grad + bufs[1 + count][rows, :]
        if last:
            loads[1 + count + adds, i].wait()
            grad = TEMP * grad
            inverse = 1.0 / norm[rows, :]
            own = bufs[1 + count + adds][rows, :] * inverse
            along = jnp.sum(own * grad, axis=1, keepdims=True)
            value = (grad - own * along) * inverse
            out[:, rows] = value.astype(BF16).T
        else:
            held[rows, :] = grad
            saves.append(pltpu.make_async_copy(held.at[rows, :], out.at[rows, :], out_sems.at[i]))
            saves[-1].start()
    for copy in saves:
        copy.wait()


def side(mine, partners, diagonal, before=None, proj=None, norm=None):
    last = proj is not None
    adds = before is not None
    args = [mine, *partners] + [before] * adds + [proj] * last
    wide = pltpu.VMEM((ROWS, D), F32)
    scratch = [pltpu.VMEM((ROWS, D), BF16)] * (1 + len(partners)) + [wide] * (adds + last) + [wide] * (not last)
    scratch += [pltpu.SemaphoreType.DMA((len(args), 2)), pltpu.SemaphoreType.DMA((2,))]
    return call(
        functools.partial(side_kernel, len(partners), diagonal, adds, last),
        "side_last" if last else "side_first",
        [HBM()] * len(args) + [VMEM()] * last,
        shape((D, ROWS), BF16) if last else shape((ROWS, D), F32),
        out_specs=VMEM() if last else HBM(),
        scratch=scratch,
        vmem=24,
    )(*args, *([norm] * last))


def loss_kernel(use_a, a_emb, b_emb, a_cross, b_cross, a_from, b_from, out):
    def total(mine, partners):
        result = jnp.zeros((1, ROWS), F32)
        for step, theirs in enumerate(partners):
            for i in range(2):
                rows = pl.ds(i * 256, 256)
                z = TEMP * lax.dot_general(theirs[rows, :], mine[...], NT, preferred_element_type=F32) + BIAS
                if step == 0:
                    row = lax.broadcasted_iota(jnp.int32, z.shape, 0) + i * 256
                    z = jnp.where(row == lax.broadcasted_iota(jnp.int32, z.shape, 1), -z, z)
                soft = jnp.maximum(z, 0.0) + jnp.log1p(jnp.exp(-jnp.abs(z)))
                result += jnp.sum(soft, axis=0, keepdims=True)
        out[...] = result

    @pl.when(use_a[0] == 1)
    def _():
        total(a_emb, (b_emb, a_cross, b_from))

    @pl.when(use_a[0] != 1)
    def _():
        total(b_emb, (a_emb, b_cross, a_from))


def head_own_kernel(grad, feats, out):
    out[...] = jnp.dot(grad[...], feats[...], preferred_element_type=F32)


def head_pack_kernel(grad, feats, before, out, held, sems):
    copies = []
    for y in range(4):
        rows = pl.ds(y * 288, 288)
        terms = before[rows, :] + jnp.dot(grad[rows, :], feats[...], preferred_element_type=F32)
        for xlo in range(2):
            for xhi in range(2):
                some = terms[xlo * 144 : xlo * 144 + 144, xhi * 384 : xhi * 384 + 384]
                chunk = 4 * y + 2 * xlo + xhi
                held[chunk, 0:144, :] = some[:, 0:128].astype(BF16)
                held[chunk, 144:288, :] = some[:, 128:256].astype(BF16)
                few = some[:, 256:384]
                few = few[0:48] + pltpu.roll(few[48:96], 32, 1) + pltpu.roll(few[96:144], 64, 1)
                held[chunk, 288:336, :] = few.astype(BF16)
        four = pl.ds(4 * y, 4)
        copies.append(pltpu.make_async_copy(held.at[four], out.at[four], sems.at[y]))
        copies[-1].start()
    for copy in copies:
        copy.wait()


def repack(total, store):
    lane = lax.broadcasted_iota(jnp.int32, (48, 128), 1)
    for z in range(8):
        value = jnp.zeros((48, 128), F32)
        for g in range(3):
            first = (z // 4) * 144 + g * 48
            wide = total[first : first + 48, :]
            turn = (32 * g - 32 * (z % 4)) % 128
            wide = pltpu.roll(wide, turn, 1) if turn else wide
            value = jnp.where((lane >= 32 * g) & (lane < 32 * g + 32), wide, value)
            few = total[288:336, :]
            turn = (96 + 4 * g - 32 * g - 4 * z) % 128
            few = pltpu.roll(few, turn, 1) if turn else few
            first = 96 + 4 * g
            value = jnp.where((lane >= first) & (lane < first + 4), few, value)
        store(z, value)


def add_y_kernel(me, got, *outs):
    for far, out in enumerate(outs):
        which = me[0] ^ far
        value = got[0, which].astype(F32)
        for s in range(1, 4):
            value = value + got[s, which].astype(F32)
        out[...] = value.astype(out.dtype)


def add_pack_kernel(odd, keep, near, cross, corner, b_got, out):
    same = keep[...] + near[...].astype(F32)
    other = cross[...].astype(F32) + corner[...].astype(F32)
    is_odd = odd[0] == 1
    for head in range(2):
        total = jnp.where(is_odd, other, same) if head == 0 else jnp.where(is_odd, same, other)
        for y in range(4):
            for xhi in range(2):
                total = total + b_got[4 * y + 2 * (1 - head) + xhi].astype(F32)

        def store(z, value, head=head):
            out[z, head] = value

        repack(total, store)


def finish_kernel(got, text, image):
    for head, out in enumerate((text, image)):
        turned = jnp.sum(got[:, head], axis=0).T
        parts = []
        for g in range(3):
            parts.append(jnp.concatenate([turned[32 * g : 32 * g + 32], turned[96 + 4 * g : 100 + 4 * g]], axis=0))
        out[...] = jnp.concatenate(parts, axis=1)


def position(coords):
    index = 0
    for coord, size in zip(coords, SIZES):
        index = index * size + coord % size
    return index


def move(value, target):
    pairs = []
    for source in range(math.prod(SIZES)):
        rest, coords = source, []
        for size in reversed(SIZES):
            coords.insert(0, rest % size)
            rest //= size
        pairs.append((source, position(target(*coords))))
    return lax.ppermute(value, AXES, pairs)


def swap_x(value):
    return move(value, lambda y, xl, xh, z, c: (y, 1 - xl, xh, z, c))


def swap_core(value):
    return move(value, lambda y, xl, xh, z, c: (y, xl, xh, z, 1 - c))


def shift_y(value, even, odd):
    return move(value, lambda y, xl, xh, z, c: (y + (odd if xl else even), xl, xh, z, c))


def after(values, *earlier):
    return lax.optimization_barrier((*values, *earlier))[: len(values)]


def core_columns(core):
    row = lax.broadcasted_iota(jnp.int32, (D, 768), 0)
    col = lax.broadcasted_iota(jnp.int32, (D, 768), 1)
    xhi, lane = col // 384, col % 384
    few = lane >= 256
    z = jnp.where(few, (lane - 256) // 4, lane // 32)
    r = jnp.where(few, 32 + (lane - 256) % 4, lane % 32)
    source = jnp.where(lane < 288, xhi * 576 + z * 72 + core * 36 + r, -1)
    return (row == source).astype(BF16)


def body(image_feats, text_feats, image_head, text_head):
    odd = lax.axis_index("xlo")
    core = lax.axis_index("core")
    flag = odd.astype(jnp.int32).reshape(1)

    a_emb, a_proj, a_norm, b_emb, b_proj, b_norm = embed(flag, image_feats, text_feats, image_head, text_head)
    a_cross = swap_x(a_emb)
    b_from = shift_y(b_emb, -1, 1)
    a_from = shift_y(a_emb, 1, -1)

    def together(steps, *args):
        def nothing(*_):
            return jax.tree.map(lambda x: jnp.zeros(x.shape, x.dtype), jax.eval_shape(steps, *args))

        return lax.cond(flag[0] < 2, steps, nothing, *args)

    def prepare(image_feats, text_feats, a_emb, b_emb):
        own_columns, oth_columns = core_columns(core), core_columns(1 - core)
        a_feats = jnp.where(odd == 1, image_feats, text_feats)
        b_feats = jnp.where(odd == 1, text_feats, image_feats)

        def columns(feats):
            own = jnp.dot(feats, own_columns, preferred_element_type=F32).astype(BF16)
            oth = jnp.dot(feats, oth_columns, preferred_element_type=F32).astype(BF16)
            return own, swap_core(oth)

        firsts = side(a_emb, (b_emb,), True), side(b_emb, (a_emb,), True)
        return (*columns(a_feats), *columns(b_feats), *firsts)

    a_own, a_oth, b_own, b_oth, a_first, b_first = together(prepare, image_feats, text_feats, a_emb, b_emb)
    (a_cross,) = after((a_cross,), a_own, b_own, a_oth, b_oth, a_first, b_first)
    (b_from,) = after((b_from,), a_cross)
    b_cross = swap_x(b_from)
    (a_first,) = after((a_first,), a_from)

    def head_terms(mine, own, oth):
        theirs = swap_core(mine)
        before = call(head_own_kernel, "head_own", [VMEM()] * 2, shape((D, 768), F32))(mine, own)
        return call(
            head_pack_kernel,
            "head_pack",
            [VMEM()] * 3,
            shape((16, 336, 128), BF16),
            out_specs=HBM(),
            scratch=[pltpu.VMEM((16, 336, 128), BF16), pltpu.SemaphoreType.DMA((4,))],
        )(theirs, oth, before)

    def finished(mine, partners, before, proj, norm, own, oth):
        return head_terms(side(mine, partners, False, before, proj, norm), own, oth)

    a_terms = together(finished, a_emb, (a_cross, b_from), a_first, a_proj, a_norm, a_own, a_oth)
    a_got = lax.all_to_all(a_terms.reshape(4, 4, 336, 128), "y", 0, 0)
    me = (2 * odd + lax.axis_index("xhi")).astype(jnp.int32).reshape(1)
    keep, near, cross, corner = call(add_y_kernel, "add_y", [SMEM(), VMEM()], [shape((336, 128), F32)] + [shape((336, 128), BF16)] * 3)(
        me, a_got
    )
    near = move(near, lambda y, xl, xh, z, c: (y, xl, 1 - xh, z, c))
    cross = move(cross, lambda y, xl, xh, z, c: (y, 1 - xl, xh, z, c))
    corner = move(corner, lambda y, xl, xh, z, c: (y, 1 - xl, 1 - xh, z, c))

    (a_from,) = after((a_from,), a_terms)
    b_first = side(b_emb, (a_from,), False, b_first)
    b_terms = together(finished, b_emb, (b_cross,), b_first, b_proj, b_norm, b_own, b_oth)
    b_got = lax.all_to_all(b_terms, ("y", "xlo", "xhi"), 0, 0)

    (loss_emb,) = after((a_emb,), b_terms)
    row_loss = call(loss_kernel, "loss", [SMEM()] + [VMEM()] * 6, shape((1, ROWS), F32))(
        flag, loss_emb, b_emb, a_cross, b_cross, a_from, b_from
    )
    (b_got,) = after((b_got,), row_loss)
    part = call(add_pack_kernel, "add_pack", [SMEM()] + [VMEM()] * 5, shape((8, 2, 48, 128), F32))(
        flag, keep, near, cross, corner, b_got
    )
    got = lax.all_to_all(part, "z", 0, 0)
    text_grad, image_grad = call(finish_kernel, "finish", [VMEM()], [shape((36, 144), F32), shape((36, 144), F32)])(got)
    return row_loss.reshape(ROWS), image_grad, text_grad


def solution(mesh):
    fine = Mesh(mesh.devices.reshape(SIZES), AXES)
    blk, dp = ("y", "xlo"), ("xhi", "z", "core")
    placed = (P(AXES, None), P(AXES, None), P(), P())
    return jax.shard_map(
        body,
        mesh=fine,
        in_specs=placed,
        out_specs=(P(AXES), P(dp, blk), P(dp, blk)),
        check_vma=False,
    )
```

```python
import functools
import math

import jax
import jax.numpy as jnp
from jax import lax
from jax.experimental import pallas as pl
from jax.experimental.pallas import tpu as pltpu
from jax.sharding import Mesh
from jax.sharding import PartitionSpec as P

TEMP = 30.0
BIAS = -6.0
EPS = 1e-06
LOG2E = math.log2(math.e)
F32 = jnp.float32
BF16 = jnp.bfloat16
D = 1152
ROWS = 512
AXES = ("y", "xlo", "xhi", "z", "core")
SIZES = (4, 2, 2, 8, 2)
MIB = 1024 * 1024
EMBED_VMEM = 52
NT = (((1,), (1,)), ((), ()))

VMEM = functools.partial(pl.BlockSpec, memory_space=pltpu.VMEM)
SMEM = functools.partial(pl.BlockSpec, memory_space=pltpu.SMEM)
HBM = functools.partial(pl.BlockSpec, memory_space=pltpu.HBM)


def shape(dims, dtype):
    return jax.ShapeDtypeStruct(dims, dtype)


def call(kernel, name, ins, outs, out_specs=None, scratch=(), vmem=20):
    if out_specs is None:
        out_specs = jax.tree.map(lambda _: VMEM(), outs)
    return pl.pallas_call(
        kernel,
        name=name,
        in_specs=ins,
        out_shape=outs,
        out_specs=out_specs,
        scratch_shapes=list(scratch),
        compiler_params=pltpu.CompilerParams(vmem_limit_bytes=vmem * MIB),
        cost_estimate=pl.CostEstimate(flops=1000, bytes_accessed=1000, transcendentals=0),
    )


def embed_kernel(odd, image_feats, text_feats, image_head, text_head, *refs):
    outs, (feats, head, held, in_sems, out_sems) = refs[:6], refs[6:]
    cuts = (pl.ds(0, 512), pl.ds(512, 512), pl.ds(1024, 128))

    def loads(side, src_feats, src_head):
        yield pltpu.make_async_copy(src_feats, feats.at[side], in_sems.at[side, 3])
        for j, cols in enumerate(cuts):
            yield pltpu.make_async_copy(src_head.at[:, cols], head.at[side, :, cols], in_sems.at[side, j])

    for value in range(2):

        @pl.when(odd[0] == value)
        def _(value=value):
            order = ((text_feats, text_head), (image_feats, image_head))
            for side in range(2):
                for copy in loads(side, *order[side ^ value]):
                    copy.start()

    saves = []
    for side in range(2):
        emb, proj_out, norm = outs[3 * side : 3 * side + 3]
        waits = list(loads(side, image_feats, image_head))
        waits[0].wait()
        total = jnp.zeros((ROWS, 1), F32)
        for j, cols in enumerate(cuts):
            waits[j + 1].wait()
            proj = jnp.dot(feats[side], head[side, :, cols], preferred_element_type=F32)
            held[side, :, cols] = proj
            saves.append(pltpu.make_async_copy(held.at[side, :, cols], proj_out.at[:, cols], out_sems.at[side, j]))
            saves[-1].start()
            total += jnp.sum(proj * proj, axis=1, keepdims=True)
        length = jnp.sqrt(total + EPS)
        norm[...] = length
        emb[...] = (held[side] * (1.0 / length)).astype(BF16)
    for copy in saves:
        copy.wait()


def embed(odd, image_feats, text_feats, image_head, text_head):
    one = [shape((ROWS, D), BF16), shape((ROWS, D), F32), shape((ROWS, 1), F32)]
    return call(
        embed_kernel,
        "embed",
        [SMEM(), HBM(), HBM(), HBM(), HBM()],
        one + one,
        out_specs=[VMEM(), HBM(), VMEM()] * 2,
        scratch=[
            pltpu.VMEM((2, ROWS, D), BF16),
            pltpu.VMEM((2, D, D), BF16),
            pltpu.VMEM((2, ROWS, D), F32),
            pltpu.SemaphoreType.DMA((2, 4)),
            pltpu.SemaphoreType.DMA((2, 3)),
        ],
        vmem=EMBED_VMEM,
    )(odd, image_feats, text_feats, image_head, text_head)


def add_pair(mine, theirs, rows, diagonal):
    dots = lax.dot_general(mine[rows, :], theirs[...], NT, preferred_element_type=F32)
    grow = dots * (-TEMP * LOG2E) + (-BIAS * LOG2E)
    if diagonal:
        row = lax.broadcasted_iota(jnp.int32, dots.shape, 0) + rows.start
        eye = row == lax.broadcasted_iota(jnp.int32, dots.shape, 1)
        grow = jnp.where(eye, -grow, grow)
    weights = 1.0 / (float(ROWS) + jnp.exp2(grow + math.log2(ROWS)))
    if diagonal:
        weights = jnp.where(eye, -weights, weights)
    return jnp.dot(weights.astype(BF16), theirs[...], preferred_element_type=F32)


def side_kernel(count, diagonal, adds, last, *refs):
    refs = list(refs)
    take = lambda number: [refs.pop(0) for _ in range(number)]
    sources = take(1 + count + adds + last)
    norm = take(1)[0] if last else None
    (out,) = take(1)
    bufs = take(len(sources))
    held = None if last else take(1)[0]
    in_sems, out_sems = refs
    block = 256
    parts = [pl.ds(i * block, block) for i in range(ROWS // block)]
    loads = {}
    for k in range(1 + count):
        loads[k] = pltpu.make_async_copy(sources[k], bufs[k], in_sems.at[k, 0])
        loads[k].start()
    for i, rows in enumerate(parts):
        for k in range(1 + count, len(sources)):
            loads[k, i] = pltpu.make_async_copy(sources[k].at[rows, :], bufs[k].at[rows, :], in_sems.at[k, i])
            loads[k, i].start()
    saves = []
    loads[0].wait()
    for i, rows in enumerate(parts):
        grad = None
        for step in range(count):
            if i == 0:
                loads[1 + step].wait()
            part = add_pair(bufs[0], bufs[1 + step], rows, diagonal and step == 0)
            grad = part if grad is None else grad + part
        if adds:
            loads[1 + count, i].wait()
            grad = grad + bufs[1 + count][rows, :]
        if last:
            loads[1 + count + adds, i].wait()
            grad = TEMP * grad
            inverse = 1.0 / norm[rows, :]
            own = bufs[1 + count + adds][rows, :] * inverse
            along = jnp.sum(own * grad, axis=1, keepdims=True)
            value = (grad - own * along) * inverse
            out[:, rows] = value.astype(BF16).T
        else:
            held[rows, :] = grad
            saves.append(pltpu.make_async_copy(held.at[rows, :], out.at[rows, :], out_sems.at[i]))
            saves[-1].start()
    for copy in saves:
        copy.wait()


def side(mine, partners, diagonal, before=None, proj=None, norm=None):
    last = proj is not None
    adds = before is not None
    args = [mine, *partners] + [before] * adds + [proj] * last
    wide = pltpu.VMEM((ROWS, D), F32)
    scratch = [pltpu.VMEM((ROWS, D), BF16)] * (1 + len(partners)) + [wide] * (adds + last) + [wide] * (not last)
    scratch += [pltpu.SemaphoreType.DMA((len(args), 2)), pltpu.SemaphoreType.DMA((2,))]
    return call(
        functools.partial(side_kernel, len(partners), diagonal, adds, last),
        "side_last" if last else "side_first",
        [HBM()] * len(args) + [VMEM()] * last,
        shape((D, ROWS), BF16) if last else shape((ROWS, D), F32),
        out_specs=VMEM() if last else HBM(),
        scratch=scratch,
        vmem=24,
    )(*args, *([norm] * last))


def loss_kernel(use_a, a_emb, b_emb, a_cross, b_cross, a_from, b_from, out):
    def total(mine, partners):
        result = jnp.zeros((1, ROWS), F32)
        for step, theirs in enumerate(partners):
            for i in range(2):
                rows = pl.ds(i * 256, 256)
                z = TEMP * lax.dot_general(theirs[rows, :], mine[...], NT, preferred_element_type=F32) + BIAS
                if step == 0:
                    row = lax.broadcasted_iota(jnp.int32, z.shape, 0) + i * 256
                    z = jnp.where(row == lax.broadcasted_iota(jnp.int32, z.shape, 1), -z, z)
                soft = jnp.maximum(z, 0.0) + jnp.log1p(jnp.exp(-jnp.abs(z)))
                result += jnp.sum(soft, axis=0, keepdims=True)
        out[...] = result

    @pl.when(use_a[0] == 1)
    def _():
        total(a_emb, (b_emb, a_cross, b_from))

    @pl.when(use_a[0] != 1)
    def _():
        total(b_emb, (a_emb, b_cross, a_from))


def head_own_kernel(grad, feats, out):
    out[...] = jnp.dot(grad[...], feats[...], preferred_element_type=F32)


def head_pack_kernel(grad, feats, before, out, held, sems):
    copies = []
    for y in range(4):
        rows = pl.ds(y * 288, 288)
        terms = before[rows, :] + jnp.dot(grad[rows, :], feats[...], preferred_element_type=F32)
        for xlo in range(2):
            for xhi in range(2):
                some = terms[xlo * 144 : xlo * 144 + 144, xhi * 384 : xhi * 384 + 384]
                chunk = 4 * y + 2 * xlo + xhi
                held[chunk, 0:144, :] = some[:, 0:128].astype(BF16)
                held[chunk, 144:288, :] = some[:, 128:256].astype(BF16)
                few = some[:, 256:384]
                few = few[0:48] + pltpu.roll(few[48:96], 32, 1) + pltpu.roll(few[96:144], 64, 1)
                held[chunk, 288:336, :] = few.astype(BF16)
        four = pl.ds(4 * y, 4)
        copies.append(pltpu.make_async_copy(held.at[four], out.at[four], sems.at[y]))
        copies[-1].start()
    for copy in copies:
        copy.wait()


def repack(total, store):
    lane = lax.broadcasted_iota(jnp.int32, (48, 128), 1)
    for z in range(8):
        value = jnp.zeros((48, 128), F32)
        for g in range(3):
            first = (z // 4) * 144 + g * 48
            wide = total[first : first + 48, :]
            turn = (32 * g - 32 * (z % 4)) % 128
            wide = pltpu.roll(wide, turn, 1) if turn else wide
            value = jnp.where((lane >= 32 * g) & (lane < 32 * g + 32), wide, value)
            few = total[288:336, :]
            turn = (96 + 4 * g - 32 * g - 4 * z) % 128
            few = pltpu.roll(few, turn, 1) if turn else few
            first = 96 + 4 * g
            value = jnp.where((lane >= first) & (lane < first + 4), few, value)
        store(z, value)


def add_y_kernel(me, got, *outs):
    for far, out in enumerate(outs):
        which = me[0] ^ far
        value = got[0, which].astype(F32)
        for s in range(1, 4):
            value = value + got[s, which].astype(F32)
        out[...] = value.astype(out.dtype)


def add_pack_kernel(odd, keep, near, cross, corner, b_got, out):
    same = keep[...] + near[...].astype(F32)
    other = cross[...].astype(F32) + corner[...].astype(F32)
    is_odd = odd[0] == 1
    for head in range(2):
        total = jnp.where(is_odd, other, same) if head == 0 else jnp.where(is_odd, same, other)
        for y in range(4):
            for xhi in range(2):
                total = total + b_got[4 * y + 2 * (1 - head) + xhi].astype(F32)

        def store(z, value, head=head):
            out[z, head] = value.astype(BF16)

        repack(total, store)


def finish_kernel(got, text, image):
    for head, out in enumerate((text, image)):
        turned = jnp.sum(got[:, head].astype(F32), axis=0).T
        parts = []
        for g in range(3):
            parts.append(jnp.concatenate([turned[32 * g : 32 * g + 32], turned[96 + 4 * g : 100 + 4 * g]], axis=0))
        out[...] = jnp.concatenate(parts, axis=1)


def position(coords):
    index = 0
    for coord, size in zip(coords, SIZES):
        index = index * size + coord % size
    return index


def move(value, target):
    pairs = []
    for source in range(math.prod(SIZES)):
        rest, coords = source, []
        for size in reversed(SIZES):
            coords.insert(0, rest % size)
            rest //= size
        pairs.append((source, position(target(*coords))))
    return lax.ppermute(value, AXES, pairs)


def swap_x(value):
    return move(value, lambda y, xl, xh, z, c: (y, 1 - xl, xh, z, c))


def swap_core(value):
    return move(value, lambda y, xl, xh, z, c: (y, xl, xh, z, 1 - c))


def shift_y(value, even, odd):
    return move(value, lambda y, xl, xh, z, c: (y + (odd if xl else even), xl, xh, z, c))


def after(values, *earlier):
    return lax.optimization_barrier((*values, *earlier))[: len(values)]


def core_columns(core):
    row = lax.broadcasted_iota(jnp.int32, (D, 768), 0)
    col = lax.broadcasted_iota(jnp.int32, (D, 768), 1)
    xhi, lane = col // 384, col % 384
    few = lane >= 256
    z = jnp.where(few, (lane - 256) // 4, lane // 32)
    r = jnp.where(few, 32 + (lane - 256) % 4, lane % 32)
    source = jnp.where(lane < 288, xhi * 576 + z * 72 + core * 36 + r, -1)
    return (row == source).astype(BF16)


def body(image_feats, text_feats, image_head, text_head):
    odd = lax.axis_index("xlo")
    core = lax.axis_index("core")
    flag = odd.astype(jnp.int32).reshape(1)

    a_emb, a_proj, a_norm, b_emb, b_proj, b_norm = embed(flag, image_feats, text_feats, image_head, text_head)
    a_cross = swap_x(a_emb)
    b_from = shift_y(b_emb, -1, 1)
    a_from = shift_y(a_emb, 1, -1)

    def together(steps, *args):
        def nothing(*_):
            return jax.tree.map(lambda x: jnp.zeros(x.shape, x.dtype), jax.eval_shape(steps, *args))

        return lax.cond(flag[0] < 2, steps, nothing, *args)

    def prepare(image_feats, text_feats, a_emb, b_emb):
        own_columns, oth_columns = core_columns(core), core_columns(1 - core)
        a_feats = jnp.where(odd == 1, image_feats, text_feats)
        b_feats = jnp.where(odd == 1, text_feats, image_feats)

        def columns(feats):
            own = jnp.dot(feats, own_columns, preferred_element_type=F32).astype(BF16)
            oth = jnp.dot(feats, oth_columns, preferred_element_type=F32).astype(BF16)
            return own, swap_core(oth)

        firsts = side(a_emb, (b_emb,), True), side(b_emb, (a_emb,), True)
        return (*columns(a_feats), *columns(b_feats), *firsts)

    a_own, a_oth, b_own, b_oth, a_first, b_first = together(prepare, image_feats, text_feats, a_emb, b_emb)
    (a_cross,) = after((a_cross,), a_own, b_own, a_oth, b_oth, a_first, b_first)
    (b_from,) = after((b_from,), a_cross)
    b_cross = swap_x(b_from)
    (a_first,) = after((a_first,), a_from)

    def head_terms(mine, own, oth):
        theirs = swap_core(mine)
        before = call(head_own_kernel, "head_own", [VMEM()] * 2, shape((D, 768), F32))(mine, own)
        return call(
            head_pack_kernel,
            "head_pack",
            [VMEM()] * 3,
            shape((16, 336, 128), BF16),
            out_specs=HBM(),
            scratch=[pltpu.VMEM((16, 336, 128), BF16), pltpu.SemaphoreType.DMA((4,))],
        )(theirs, oth, before)

    def finished(mine, partners, before, proj, norm, own, oth):
        return head_terms(side(mine, partners, False, before, proj, norm), own, oth)

    a_terms = together(finished, a_emb, (a_cross, b_from), a_first, a_proj, a_norm, a_own, a_oth)
    a_got = lax.all_to_all(a_terms.reshape(4, 4, 336, 128), "y", 0, 0)
    me = (2 * odd + lax.axis_index("xhi")).astype(jnp.int32).reshape(1)
    keep, near, cross, corner = call(add_y_kernel, "add_y", [SMEM(), VMEM()], [shape((336, 128), F32)] + [shape((336, 128), BF16)] * 3)(
        me, a_got
    )
    near = move(near, lambda y, xl, xh, z, c: (y, xl, 1 - xh, z, c))
    cross = move(cross, lambda y, xl, xh, z, c: (y, 1 - xl, xh, z, c))
    corner = move(corner, lambda y, xl, xh, z, c: (y, 1 - xl, 1 - xh, z, c))

    (a_from,) = after((a_from,), a_terms)
    b_first = side(b_emb, (a_from,), False, b_first)
    b_terms = together(finished, b_emb, (b_cross,), b_first, b_proj, b_norm, b_own, b_oth)
    b_got = lax.all_to_all(b_terms, ("y", "xlo", "xhi"), 0, 0)

    (loss_emb,) = after((a_emb,), b_terms)
    row_loss = call(loss_kernel, "loss", [SMEM()] + [VMEM()] * 6, shape((1, ROWS), F32))(
        flag, loss_emb, b_emb, a_cross, b_cross, a_from, b_from
    )
    (b_got,) = after((b_got,), row_loss)
    part = call(add_pack_kernel, "add_pack", [SMEM()] + [VMEM()] * 5, shape((8, 2, 48, 128), BF16))(
        flag, keep, near, cross, corner, b_got
    )
    got = lax.all_to_all(part, "z", 0, 0)
    text_grad, image_grad = call(finish_kernel, "finish", [VMEM()], [shape((36, 144), F32), shape((36, 144), F32)])(got)
    return row_loss.reshape(ROWS), image_grad, text_grad


def solution(mesh):
    fine = Mesh(mesh.devices.reshape(SIZES), AXES)
    blk, dp = ("y", "xlo"), ("xhi", "z", "core")
    placed = (P(AXES, None), P(AXES, None), P(), P())
    return jax.shard_map(
        body,
        mesh=fine,
        in_specs=placed,
        out_specs=(P(AXES), P(dp, blk), P(dp, blk)),
        check_vma=False,
    )
```
